32 devices in a mesh: seq: 2 (over x), fsdp: 4 (over z), replica: 4 (over y, core).
Axes of the slice: x: 2, y: 2, z: 4, core: 2. Of those that a mesh axis runs over, the one named last changes fastest.
Arguments:
- latent_tokens: bfloat16 [32, 1024, 1152], P(('fsdp', 'replica'), 'seq'), may hold values from -6 to 6
- conditioning: bfloat16 [32, 1152], P(('fsdp', 'replica')), may hold values from -6 to 6
- ada_weight: bfloat16 [1152, 6912], P(('seq', 'fsdp')), may hold values from -0.1875 to 0.1875
- ada_bias: bfloat16 [6912], P(('seq', 'fsdp')), may hold values from -2 to 2
- qkv_weight: bfloat16 [1152, 3456], P(('seq', 'fsdp')), may hold values from -0.1875 to 0.1875
- qv_bias: bfloat16 [2304], P(('seq', 'fsdp')), may hold values from -2 to 2
- out_weight: bfloat16 [1152, 1152], P(('seq', 'fsdp')), may hold values from -3 to 3
- out_bias: bfloat16 [1152], P(('seq', 'fsdp')), may hold values from -2 to 2
- up_weight: bfloat16 [1152, 4608], P(('seq', 'fsdp')), may hold values from -0.1875 to 0.1875
- up_bias: bfloat16 [4608], P(('seq', 'fsdp')), may hold values from -2 to 2
- down_weight: bfloat16 [4608, 1152], P(('seq', 'fsdp')), may hold values from -0.09375 to 0.09375
- down_bias: bfloat16 [1152], P(('seq', 'fsdp')), may hold values from -2 to 2
- out_cotangent: bfloat16 [32, 1024, 1152], P(('fsdp', 'replica'), 'seq'), may hold values from -6 to 6
Outputs:
- block_out: bfloat16 [32, 1024, 1152], P(('fsdp', 'replica'), 'seq')
- tokens_grad: float32 [32, 1024, 1152], P(('fsdp', 'replica'), 'seq')
- cond_grad: float32 [32, 1152], P(('fsdp', 'replica'))
- ada_wgrad: float32 [1152, 6912], P(('seq', 'fsdp'))
- ada_bgrad: float32 [6912], P(('seq', 'fsdp'))
- qkv_wgrad: float32 [1152, 3456], P(('seq', 'fsdp'))
- qv_bgrad: float32 [2304], P(('seq', 'fsdp'))
- out_wgrad: float32 [1152, 1152], P(('seq', 'fsdp'))
- out_bgrad: float32 [1152], P(('seq', 'fsdp'))
- up_wgrad: float32 [1152, 4608], P(('seq', 'fsdp'))
- up_bgrad: float32 [4608], P(('seq', 'fsdp'))
- down_wgrad: float32 [4608, 1152], P(('seq', 'fsdp'))
- down_bgrad: float32 [1152], P(('seq', 'fsdp'))
The draws below stay inside these ranges and needn't reach their ends.
All inputs are finite; a program needn't handle non-finite values.
Results may differ from the reference program's by a relative error of at most 0.02.
The reference program's roundings to bfloat16 on the way count: a program that leaves them out, or rounds other values in their place, can miss the bound.
Values may be sent and summed in bfloat16 or wider, within the bound.
A program may use at most 384 MiB of HBM per device.

```python
import math
import jax
import jax.numpy as jnp
from jax import lax

D = 1152
FF = 4608
HEADS = 16
HEAD_DIM = 72
SEQ_LEN = 1024
LATENTS = 32


def levels(rng, dims, cuts, least, largest):
    def one(axis_at, shards_of):
        steps = jax.random.uniform(jax.random.fold_in(jax.random.fold_in(rng, 6), axis_at), (shards_of,), jnp.float32, least / len(cuts), largest / len(cuts))
        return jnp.repeat(jnp.exp(steps), dims[axis_at] // shards_of).reshape((-1,) + (1,) * (len(dims) - axis_at - 1))

    level = one(*cuts[0])
    for cut in cuts[1:]:
        level = level * one(*cut)
    return level


def centred(stream_key, extent, deviation, bound, cuts=(), held_as=jnp.bfloat16):
    loudness = levels(stream_key, extent, cuts, -0.22, 0.18) if cuts else 1.0
    array = jax.random.normal(stream_key, extent, jnp.float32) * deviation * loudness
    return jnp.minimum(jnp.maximum(array, -bound), bound).astype(held_as)


def setup_inputs(seed: int = 0) -> dict:
    arg_keys = jax.random.split(jax.random.key(seed), 14)
    return {
        "latent_tokens": centred(arg_keys[0], (LATENTS, SEQ_LEN, D), 1.0, 6.0, ((0, 16), (1, 2))),
        "conditioning": centred(arg_keys[1], (LATENTS, D), 1.0, 6.0, ((0, 16),)),
        "ada_weight": centred(arg_keys[2], (D, 6 * D), D ** -0.5, 0.1875, ((0, 8),)),
        "ada_bias": centred(arg_keys[3], (6 * D,), 0.3, 2.0, ((0, 8),)),
        "qkv_weight": centred(arg_keys[4], (D, 3 * D), D ** -0.5, 0.1875, ((0, 8),)),
        "qv_bias": centred(arg_keys[5], (2 * D,), 0.3, 2.0, ((0, 8),)),
        "out_weight": centred(arg_keys[6], (D, D), (max(1, D * 4 // SEQ_LEN)) ** -0.5, 3.0, ((0, 8),)),
        "out_bias": centred(arg_keys[7], (D,), 0.3, 2.0, ((0, 8),)),
        "up_weight": centred(arg_keys[8], (D, FF), D ** -0.5, 0.1875, ((0, 8),)),
        "up_bias": centred(arg_keys[9], (FF,), 0.3, 2.0, ((0, 8),)),
        "down_weight": centred(arg_keys[10], (FF, D), FF ** -0.5, 0.09375, ((0, 8),)),
        "down_bias": centred(arg_keys[11], (D,), 0.3, 2.0, ((0, 8),)),
        "out_cotangent": centred(arg_keys[12], (LATENTS, SEQ_LEN, D), 1.0, 6.0, ((0, 16), (1, 2))),
    }


@jax.custom_vjp
def low(v):
    return lax.optimization_barrier(v.astype(jnp.bfloat16)).astype(jnp.float32)

@jax.custom_vjp
def low_back(v):
    return v

def low_keep(v):
    return (low(v), None)

def low_pass(kept, grad):
    return (grad,)

def back_keep(v):
    return (v, None)

def back_low(kept, grad):
    return (low(grad),)
low.defvjp(low_keep, low_pass)
low_back.defvjp(back_keep, back_low)

def layer_norm(values):
    centre = values - lax.optimization_barrier(jnp.mean(values, axis=-1, keepdims=True))
    spread = lax.optimization_barrier(jnp.mean(centre * centre, axis=-1, keepdims=True))
    return centre * lax.rsqrt(spread + 1e-06)

def latent_block(weights, tokens, cond):
    highest = lax.Precision.HIGHEST
    w_ada, b_ada, w_qkv, b_qv, w_out, b_out, w_up, b_up, w_down, b_down = weights
    activated = low(jax.nn.silu(cond))
    modulation = low_back(jnp.dot(activated, w_ada, precision=highest) + b_ada)
    shift_a, scale_a, gate_a, shift_m, scale_m, gate_m = jnp.split(modulation, 6)
    attn_in = low(layer_norm(tokens) * (1.0 + scale_a) + shift_a)
    bias_full = jnp.concatenate([b_qv[:D], jnp.zeros((D,), jnp.float32), b_qv[D:]])
    projected = low(low_back(jnp.dot(attn_in, w_qkv, precision=highest) + bias_full))
    query = projected[:, :D].reshape(SEQ_LEN, HEADS, HEAD_DIM)
    keys = projected[:, D:2 * D].reshape(SEQ_LEN, HEADS, HEAD_DIM)
    values = projected[:, 2 * D:].reshape(SEQ_LEN, HEADS, HEAD_DIM)
    scale_factor = 1.0 / math.sqrt(HEAD_DIM)
    scores = low_back(jnp.einsum('qhd,khd->hqk', query, keys, precision=highest) * scale_factor)
    probs = low(jax.nn.softmax(scores, axis=-1))
    attended = jnp.einsum('hqk,khd->qhd', probs, values, precision=highest).reshape(SEQ_LEN, D)
    attended = low(low_back(attended))
    branch = low_back(jnp.dot(attended, w_out, precision=highest) + b_out)
    middle = tokens + gate_a * branch
    mlp_in = low(layer_norm(middle) * (1.0 + scale_m) + shift_m)
    pre_act = low_back(jnp.dot(mlp_in, w_up, precision=highest) + b_up)
    hidden = low(jax.nn.gelu(pre_act, approximate=True))
    mlp_out = low_back(jnp.dot(hidden, w_down, precision=highest) + b_down)
    return middle + gate_m * mlp_out

def reference(latent_tokens, conditioning, ada_weight, ada_bias, qkv_weight, qv_bias, out_weight, out_bias, up_weight, up_bias, down_weight, down_bias, out_cotangent):
    weights = tuple((w.astype(jnp.float32) for w in (ada_weight, ada_bias, qkv_weight, qv_bias, out_weight, out_bias, up_weight, up_bias, down_weight, down_bias)))
    tokens32 = latent_tokens.astype(jnp.float32)
    cond32 = conditioning.astype(jnp.float32)
    cotangent = out_cotangent.astype(jnp.float32)
    group = math.gcd(LATENTS, max(1, 4096 // SEQ_LEN))

    def whole(weight_set, tokens, cond):
        token_groups = tokens.reshape(LATENTS // group, group, SEQ_LEN, D)
        cond_groups = cond.reshape(LATENTS // group, group, D)

        def one_group(pair):
            return jax.vmap(lambda tok, con: latent_block(weight_set, tok, con))(pair[0], pair[1])
        result = lax.map(jax.checkpoint(one_group), (token_groups, cond_groups))
        return result.reshape(LATENTS, SEQ_LEN, D)
    output, pullback = jax.vjp(whole, weights, tokens32, cond32)
    weight_grads, tokens_grad, cond_grad = pullback(cotangent)
    return (output.astype(jnp.bfloat16), tokens_grad, cond_grad, weight_grads[0], weight_grads[1], weight_grads[2], weight_grads[3], weight_grads[4], weight_grads[5], weight_grads[6], weight_grads[7], weight_grads[8], weight_grads[9])
```

```python
import functools
import math

import jax
import jax.numpy as jnp
from jax import lax
from jax.experimental import pallas as pl
from jax.experimental.pallas import tpu as pltpu
from jax.sharding import PartitionSpec as P

HEADS = 16
HEAD_DIM = 72
PAIR = 2
PAIRS = HEADS // PAIR
ROWS = PAIR * HEAD_DIM
OWNERS = ("seq", "fsdp")
EVERY = ("seq", "fsdp", "replica")
SCALE = 1.0 / math.sqrt(HEAD_DIM)
SCALE2 = SCALE * math.log2(math.e)


def norm_mod(values, shift, scale):
    centre = values - jnp.mean(values, axis=-1, keepdims=True)
    spread = jnp.mean(centre * centre, axis=-1, keepdims=True)
    return centre * lax.rsqrt(spread + 1e-06) * (1.0 + scale) + shift


def gelu_tanh(values):
    return jax.nn.gelu(values, approximate=True)


def mm(left, right, dims):
    return lax.dot_general(left, right, (dims, ((), ())), preferred_element_type=jnp.float32)


def forward_kernel(parts, *refs):
    q_ref, k_refs, v_refs = refs[0], refs[1 : 1 + parts], refs[1 + parts : 1 + 2 * parts]
    out_ref, log_ref = refs[1 + 2 * parts :]
    outs, logs = [], []
    for head in range(PAIR):
        rows = slice(head * HEAD_DIM, (head + 1) * HEAD_DIM)
        query = q_ref[0][rows]
        scores = [mm(k[0][rows], query, ((0,), (0,))) * SCALE2 for k in k_refs]
        top = functools.reduce(jnp.maximum, [jnp.max(s, axis=0, keepdims=True) for s in scores])
        expo = [jnp.exp2(s - top) for s in scores]
        total = functools.reduce(jnp.add, [jnp.sum(e, axis=0, keepdims=True) for e in expo])
        inverse = 1.0 / total
        outs.append(
            sum(
                mm(v[0][rows], (e * inverse).astype(jnp.bfloat16), ((1,), (0,)))
                for v, e in zip(v_refs, expo)
            )
        )
        logs.append(top + jnp.log2(total))
    out_ref[0] = jnp.concatenate(outs, axis=0).astype(out_ref.dtype)
    log_ref[0, 0] = jnp.concatenate(logs, axis=0)


def backward_kernel(parts, *refs):
    q_ref, k_refs, v_refs = refs[0], refs[1 : 1 + parts], refs[1 + parts : 1 + 2 * parts]
    g_ref, log_ref = refs[1 + 2 * parts : 3 + 2 * parts]
    dq_ref, dk_refs, dv_refs = (
        refs[3 + 2 * parts],
        refs[4 + 2 * parts : 4 + 3 * parts],
        refs[4 + 3 * parts :],
    )
    dqs, dks, dvs = [], [[] for _ in range(parts)], [[] for _ in range(parts)]
    for head in range(PAIR):
        rows = slice(head * HEAD_DIM, (head + 1) * HEAD_DIM)
        query, grad = q_ref[0][rows], g_ref[0][rows]
        log_total = log_ref[0, 0, head : head + 1, :]
        probs, weighted = [], []
        for part in range(parts):
            scores = mm(k_refs[part][0][rows], query, ((0,), (0,))) * SCALE2
            prob = jnp.exp2(scores - log_total)
            d_prob = mm(v_refs[part][0][rows], grad, ((0,), (0,)))
            probs.append(prob)
            weighted.append(d_prob)
            dvs[part].append(mm(grad, prob.astype(jnp.bfloat16), ((1,), (1,))))
        delta = sum(jnp.sum(p * d, axis=0, keepdims=True) for p, d in zip(probs, weighted))
        d_query = 0.0
        for part in range(parts):
            d_score = (probs[part] * (weighted[part] - delta)).astype(jnp.bfloat16)
            d_query = d_query + mm(k_refs[part][0][rows], d_score, ((1,), (0,)))
            dks[part].append(mm(query, d_score, ((1,), (1,))) * SCALE)
        dqs.append(d_query * SCALE)
    dq_ref[0] = jnp.concatenate(dqs, axis=0).astype(dq_ref.dtype)
    for part in range(parts):
        dk_refs[part][0] = jnp.concatenate(dks[part], axis=0).astype(dq_ref.dtype)
        dv_refs[part][0] = jnp.concatenate(dvs[part], axis=0).astype(dq_ref.dtype)


def block(tokens, offset):
    return pl.BlockSpec((1, ROWS, tokens), lambda latent, pair: (latent, pair + offset, 0))


def attend_forward(projected, others):
    latents, width3, tokens = projected.shape
    width = width3 // 3
    parts = 1 + len(others)
    k_specs = [block(tokens, PAIRS)] + [block(tokens, 0)] * len(others)
    v_specs = [block(tokens, 2 * PAIRS)] + [block(tokens, PAIRS)] * len(others)
    log_spec = pl.BlockSpec((1, 1, PAIR, tokens), lambda latent, pair: (latent, pair, 0, 0))
    work = latents * HEADS * tokens * tokens * parts
    return pl.pallas_call(
        functools.partial(forward_kernel, parts),
        grid=(latents, PAIRS),
        in_specs=[block(tokens, 0)] + k_specs + v_specs,
        out_specs=[block(tokens, 0), log_spec],
        out_shape=[
            jax.ShapeDtypeStruct((latents, width, tokens), jnp.bfloat16),
            jax.ShapeDtypeStruct((latents, PAIRS, PAIR, tokens), jnp.float32),
        ],
        compiler_params=pltpu.CompilerParams(vmem_limit_bytes=40 * 1024 * 1024),
        cost_estimate=pl.CostEstimate(
            flops=12 * 128 * work, bytes_accessed=8 * projected.size, transcendentals=work
        ),
    )(projected, projected, *others, projected, *others)


def attend_backward(projected, others, grad, log_total):
    latents, width3, tokens = projected.shape
    width = width3 // 3
    parts = 1 + len(others)
    k_specs = [block(tokens, PAIRS)] + [block(tokens, 0)] * len(others)
    v_specs = [block(tokens, 2 * PAIRS)] + [block(tokens, PAIRS)] * len(others)
    log_spec = pl.BlockSpec((1, 1, PAIR, tokens), lambda latent, pair: (latent, pair, 0, 0))
    work = latents * HEADS * tokens * tokens * parts
    outs = pl.pallas_call(
        functools.partial(backward_kernel, parts),
        grid=(latents, PAIRS),
        in_specs=[block(tokens, 0)] + k_specs + v_specs + [block(tokens, 0), log_spec],
        out_specs=[block(tokens, 0)] * (1 + 2 * parts),
        out_shape=[jax.ShapeDtypeStruct((latents, width, tokens), jnp.bfloat16)] * (1 + 2 * parts),
        compiler_params=pltpu.CompilerParams(vmem_limit_bytes=48 * 1024 * 1024),
        cost_estimate=pl.CostEstimate(
            flops=30 * 128 * work, bytes_accessed=16 * projected.size, transcendentals=work
        ),
    )(projected, projected, *others, projected, *others, grad, log_total)
    return outs[0], outs[1 : 1 + parts], outs[1 + parts :]


def gather_blocks(weight, width):
    rows, cols = weight.shape
    if cols != width * lax.axis_size("replica"):
        return lax.all_gather(weight, OWNERS, axis=0, tiled=True)
    mine = lax.dynamic_slice_in_dim(weight, lax.axis_index("replica") * width, width, 1)
    blocks = lax.all_gather(mine, EVERY, axis=0, tiled=True)
    blocks = blocks.reshape(-1, cols // width, rows, width)
    return jnp.swapaxes(blocks, 1, 2).reshape(-1, cols)


def gather_rows(weight, width):
    rows, count = weight.shape[0], lax.axis_size("replica")
    if rows % (16 * count):
        return lax.all_gather(weight, OWNERS, axis=0, tiled=True)
    share = rows // count
    mine = lax.dynamic_slice_in_dim(weight, lax.axis_index("replica") * share, share, 0)
    return lax.all_gather(mine, EVERY, axis=0, tiled=True)


def sum_plain(term):
    owned = lax.psum_scatter(term, OWNERS, scatter_dimension=0, tiled=True)
    return lax.psum(owned, "replica")


def sum_blocks(term, width):
    cols, count, owners = term.shape[1], lax.axis_size("replica"), lax.axis_size(OWNERS)
    if cols != width * count:
        return sum_plain(term)
    blocks = jnp.swapaxes(term.reshape(owners, -1, count, width), 1, 2).reshape(-1, width)
    owned = lax.psum_scatter(blocks, EVERY, scatter_dimension=0, tiled=True)
    owned = lax.all_gather(owned, "replica", axis=0, tiled=False)
    return jnp.swapaxes(owned, 0, 1).reshape(-1, cols)


def sum_rows(term):
    if term.shape[0] % (16 * lax.axis_size(EVERY)):
        return sum_plain(term)
    owned = lax.psum_scatter(term, EVERY, scatter_dimension=0, tiled=True)
    return lax.all_gather(owned, "replica", axis=0, tiled=True)


def shift_seq(values, step):
    count = lax.axis_size("seq")
    return lax.ppermute(values, "seq", [(i, (i + step) % count) for i in range(count)])


def bias_term(grad, axes):
    return jnp.sum(grad.astype(jnp.float32), axis=axes)


def body(
    latent_tokens,
    conditioning,
    ada_weight,
    ada_bias,
    qkv_weight,
    qv_bias,
    out_weight,
    out_bias,
    up_weight,
    up_bias,
    down_weight,
    down_bias,
    out_cotangent,
):
    width = latent_tokens.shape[2]
    latents = latent_tokens.shape[0]
    seq_size, fsdp_size = lax.axis_size("seq"), lax.axis_size("fsdp")
    replica_size = lax.axis_size("replica")
    owner = lax.axis_index("seq") * fsdp_size + lax.axis_index("fsdp")
    owners = seq_size * fsdp_size
    fsdp_at, replica_at = lax.axis_index("fsdp"), lax.axis_index("replica")
    wide = ada_weight.shape[1]
    ada_rows = ada_weight.shape[0]

    cond32 = conditioning.astype(jnp.float32)
    activated = jax.nn.silu(cond32).astype(jnp.bfloat16)
    act_all = lax.all_gather(activated, ("fsdp", "replica"), axis=0, tiled=True)
    act_rows = lax.dynamic_slice_in_dim(act_all, owner * ada_rows, ada_rows, 1)

    def of_group(values):
        split = values.reshape((fsdp_size, replica_size, latents) + values.shape[1:])
        return lax.dynamic_index_in_dim(split, replica_at, 1, keepdims=False)

    act_group = of_group(act_rows).reshape(fsdp_size * latents, ada_rows)
    partial_mod = jnp.dot(act_group, ada_weight, preferred_element_type=jnp.float32)

    def placed(bias):
        zeros = jnp.zeros((owners * bias.shape[0],), jnp.float32)
        return lax.dynamic_update_slice_in_dim(
            zeros, bias.astype(jnp.float32), owner * bias.shape[0], 0
        )

    partial_mod = partial_mod + placed(ada_bias)[None, :]
    biases = jnp.concatenate([placed(b) for b in (qv_bias, out_bias, up_bias, down_bias)])
    bias_rows = -(-biases.shape[0] // wide)
    biases = jnp.pad(biases, (0, bias_rows * wide - biases.shape[0])).reshape(bias_rows, wide)
    small = lax.psum(jnp.concatenate([partial_mod, biases], axis=0), OWNERS)
    modulation = lax.dynamic_slice_in_dim(small, fsdp_at * latents, latents, 0)
    flat = small[fsdp_size * latents :].reshape(-1)
    hidden_units = up_weight.shape[1]
    b_qv = flat[: 2 * width]
    b_out = flat[2 * width : 3 * width]
    b_up = flat[3 * width : 3 * width + hidden_units]
    b_down = flat[3 * width + hidden_units : 4 * width + hidden_units]

    w_attn = gather_blocks(jnp.concatenate([qkv_weight, out_weight], axis=1), width)
    w_qkv, w_out = w_attn[:, : 3 * width], w_attn[:, 3 * width :]
    w_up = gather_blocks(up_weight, width)
    w_down = gather_rows(down_weight, width)

    pieces = [modulation[:, None, index * width : (index + 1) * width] for index in range(6)]
    shift_a, scale_a, gate_a, shift_m, scale_m, gate_m = pieces
    tokens32 = latent_tokens.astype(jnp.float32)
    attn_in = norm_mod(tokens32, shift_a, scale_a).astype(jnp.bfloat16)
    bias_full = jnp.concatenate([b_qv[:width], jnp.zeros((width,), jnp.float32), b_qv[width:]])

    def ein(form, left, right):
        return jnp.einsum(form, left, right, preferred_element_type=jnp.float32)

    projected = (ein("ltd,de->let", attn_in, w_qkv) + bias_full[None, :, None]).astype(jnp.bfloat16)
    own_kv = projected[:, width:, :]
    others = [shift_seq(own_kv, step) for step in range(1, seq_size)]
    attended, log_total = attend_forward(projected, others)
    branch = ein("ldt,de->lte", attended, w_out) + b_out
    middle = tokens32 + gate_a * branch
    mlp_in = norm_mod(middle, shift_m, scale_m).astype(jnp.bfloat16)
    pre_act = ein("ltd,de->lte", mlp_in, w_up) + b_up
    hidden = gelu_tanh(pre_act).astype(jnp.bfloat16)
    mlp_out = ein("ltd,de->lte", hidden, w_down) + b_down
    block_out = (middle + gate_m * mlp_out).astype(jnp.bfloat16)

    grad_out = out_cotangent.astype(jnp.float32)
    d_gate_m = jnp.sum(grad_out * mlp_out, axis=1, keepdims=True)
    d_mlp_out = (grad_out * gate_m).astype(jnp.bfloat16)
    down_term = ein("ltd,lte->de", hidden, d_mlp_out).astype(jnp.bfloat16)
    down_bias_term = bias_term(d_mlp_out, (0, 1))
    down_term, d_mlp_out = lax.optimization_barrier((down_term, d_mlp_out))
    down_grad = sum_rows(down_term)
    d_hidden = ein("lte,de->ltd", d_mlp_out, w_down)
    unused_value, gelu_pull = jax.vjp(gelu_tanh, pre_act)
    d_pre = gelu_pull(d_hidden)[0].astype(jnp.bfloat16)
    up_term = ein("ltd,lte->de", mlp_in, d_pre).astype(jnp.bfloat16)
    up_bias_term = bias_term(d_pre, (0, 1))
    up_term, d_pre = lax.optimization_barrier((up_term, d_pre))
    up_grad = sum_blocks(up_term, width)
    d_mlp_in = ein("lte,de->ltd", d_pre, w_up)
    unused_norm, norm_pull_m = jax.vjp(norm_mod, middle, shift_m, scale_m)
    d_middle_part, d_shift_m, d_scale_m = norm_pull_m(d_mlp_in)
    d_middle = grad_out + d_middle_part
    d_gate_a = jnp.sum(d_middle * branch, axis=1, keepdims=True)
    d_branch = (d_middle * gate_a).astype(jnp.bfloat16)
    out_term = ein("ldt,lte->de", attended, d_branch).astype(jnp.bfloat16)
    out_bias_term = bias_term(d_branch, (0, 1))
    out_term, d_branch = lax.optimization_barrier((out_term, d_branch))
    d_attended = ein("lte,de->ldt", d_branch, w_out).astype(jnp.bfloat16)
    d_query, d_key_parts, d_value_parts = attend_backward(projected, others, d_attended, log_total)
    d_kv = jnp.concatenate([d_key_parts[0], d_value_parts[0]], axis=1).astype(jnp.float32)
    for step in range(1, seq_size):
        there = jnp.concatenate([d_key_parts[step], d_value_parts[step]], axis=1)
        d_kv = d_kv + shift_seq(there, -step).astype(jnp.float32)
    d_projected = jnp.concatenate([d_query, d_kv.astype(jnp.bfloat16)], axis=1)
    qkv_term = ein("ltd,let->de", attn_in, d_projected).astype(jnp.bfloat16)
    projected_sums = bias_term(d_projected, (0, 2))
    qv_bias_term = jnp.concatenate([projected_sums[:width], projected_sums[2 * width :]])
    qkv_term, d_projected = lax.optimization_barrier((qkv_term, d_projected))
    attn_grad = sum_blocks(jnp.concatenate([qkv_term, out_term], axis=1), width)
    qkv_grad, out_grad = attn_grad[:, : 3 * width], attn_grad[:, 3 * width :]
    d_attn_in = ein("let,de->ltd", d_projected, w_qkv)
    unused_first, norm_pull_a = jax.vjp(norm_mod, tokens32, shift_a, scale_a)
    d_tokens_part, d_shift_a, d_scale_a = norm_pull_a(d_attn_in)
    tokens_grad = d_middle + d_tokens_part
    d_mod_part = jnp.concatenate(
        [d_shift_a, d_scale_a, d_gate_a, d_shift_m, d_scale_m, d_gate_m], axis=-1
    )[:, 0, :]
    bias_terms = jnp.concatenate([qv_bias_term, out_bias_term, up_bias_term, down_bias_term])
    bias_terms = jnp.pad(bias_terms, (0, bias_rows * wide - bias_terms.shape[0]))
    mine = jnp.concatenate([d_mod_part, bias_terms.reshape(bias_rows, wide)], axis=0)
    every = lax.all_gather(mine.astype(jnp.bfloat16), EVERY, axis=0, tiled=False)
    every = every.astype(jnp.float32)
    d_modulation = jnp.sum(
        every[:, :latents].reshape((seq_size, -1, wide)), axis=0
    ).astype(jnp.bfloat16)
    bias_sums = jnp.sum(every[:, latents:], axis=0).reshape(-1)
    ada_wgrad = jnp.einsum("ld,le->de", act_rows, d_modulation, preferred_element_type=jnp.float32)

    def owned(values, start, count):
        return lax.dynamic_slice_in_dim(values, start + owner * (count // owners), count // owners, 0)

    ada_bgrad = owned(jnp.sum(d_modulation.astype(jnp.float32), axis=0), 0, wide)
    qv_bgrad = owned(bias_sums, 0, 2 * width)
    out_bgrad = owned(bias_sums, 2 * width, width)
    up_bgrad = owned(bias_sums, 3 * width, hidden_units)
    down_bgrad = owned(bias_sums, 3 * width + hidden_units, width)

    d_group = of_group(d_modulation).reshape(fsdp_size * latents, wide)
    cond_part = jnp.einsum("le,de->ld", d_group, ada_weight, preferred_element_type=jnp.float32)
    cond_parts = lax.all_gather(cond_part, OWNERS, axis=0, tiled=False)
    cond_mine = lax.dynamic_slice_in_dim(cond_parts, fsdp_at * latents, latents, 1)
    cond_mine = jnp.swapaxes(cond_mine, 0, 1).reshape(latents, -1)
    sigmoid_cond = jax.nn.sigmoid(cond32)
    silu_slope = sigmoid_cond * (1.0 + cond32 * (1.0 - sigmoid_cond))
    cond_grad = cond_mine * silu_slope
    return (
        block_out,
        tokens_grad,
        cond_grad,
        ada_wgrad,
        ada_bgrad,
        qkv_grad.astype(jnp.float32),
        qv_bgrad,
        out_grad.astype(jnp.float32),
        out_bgrad,
        up_grad.astype(jnp.float32),
        up_bgrad,
        down_grad.astype(jnp.float32),
        down_bgrad,
    )


def solution(mesh):
    in_specs = (
        P(("fsdp", "replica"), "seq", None),
        P(("fsdp", "replica"), None),
        P(("seq", "fsdp"), None),
        P(("seq", "fsdp")),
        P(("seq", "fsdp"), None),
        P(("seq", "fsdp")),
        P(("seq", "fsdp"), None),
        P(("seq", "fsdp")),
        P(("seq", "fsdp"), None),
        P(("seq", "fsdp")),
        P(("seq", "fsdp"), None),
        P(("seq", "fsdp")),
        P(("fsdp", "replica"), "seq", None),
    )
    out_specs = (
        P(("fsdp", "replica"), "seq", None),
        P(("fsdp", "replica"), "seq", None),
        P(("fsdp", "replica"), None),
        P(("seq", "fsdp"), None),
        P(("seq", "fsdp")),
        P(("seq", "fsdp"), None),
        P(("seq", "fsdp")),
        P(("seq", "fsdp"), None),
        P(("seq", "fsdp")),
        P(("seq", "fsdp"), None),
        P(("seq", "fsdp")),
        P(("seq", "fsdp"), None),
        P(("seq", "fsdp")),
    )
    return jax.shard_map(body, mesh=mesh, in_specs=in_specs, out_specs=out_specs, check_vma=False)
```
